128 devices in a mesh: dp: 4 (over z_hi, core), seq: 32 (over y, z_lo, x).
Axes of the slice: x: 4, y: 4, z: 4 (z_hi: 2, z_lo: 2; z = z_hi * 2 + z_lo), core: 2. Of those that a mesh axis runs over, the one named last changes fastest.
Arguments:
- q_space: bfloat16 [128, 512, 2048], P(('dp', 'seq')), parts along dimension 0, may hold values from -6 to 6
- k_space: bfloat16 [128, 512, 2048], P(('dp', 'seq')), parts along dimension 0, may hold values from -6 to 6
- v_space: bfloat16 [128, 512, 2048], P(('dp', 'seq')), parts along dimension 0, may hold values from -6 to 6
- q_time: bfloat16 [128, 512, 2048], P(('dp', 'seq')), parts along dimension 0, may hold values from -6 to 6
- k_time: bfloat16 [128, 512, 2048], P(('dp', 'seq')), parts along dimension 0, may hold values from -6 to 6
- grad_out: bfloat16 [128, 512, 2048], P(('dp', 'seq')), parts along dimension 0, may hold values from -6 to 6
Outputs:
- grad_q_space: bfloat16 [128, 512, 2048], P(('dp', 'seq')), parts along dimension 0
- grad_k_space: bfloat16 [128, 512, 2048], P(('dp', 'seq')), parts along dimension 0
- grad_v_space: bfloat16 [128, 512, 2048], P(('dp', 'seq')), parts along dimension 0
- grad_q_time: bfloat16 [128, 512, 2048], P(('dp', 'seq')), parts along dimension 0
- grad_k_time: bfloat16 [128, 512, 2048], P(('dp', 'seq')), parts along dimension 0
The draws below stay inside these ranges and needn't reach their ends.
There are 4 independent parts, one for each index of `dp`. The reference program is written for one: setup_inputs(seed, part) draws one part's arguments, and reference() takes and returns one part's arrays. A program takes and returns all parts, laid end to end along the dimension named above; each array names one. Nothing has to cross between parts.
All inputs are finite; a program needn't handle non-finite values.
Results may differ from the reference program's by a relative error of at most 0.0092.
Values may be sent and summed in bfloat16 or wider, within the bound.
A program may use at most 192 MiB of HBM per device.

```python
import jax
import jax.numpy as jnp
from jax import lax

HEADS = 16
HEAD_DIM = 128
FRAMES = 32
POS = 512


def drawn_draw(key):
    return jnp.clip(jax.random.normal(key, (FRAMES, POS, HEADS * HEAD_DIM), jnp.float32), -4.0, 4.0)


def draw_q_space(key, part):
    key = jax.random.fold_in(key, 1)
    return drawn_draw(key).astype(jnp.bfloat16)


def draw_k_space(key, part):
    key = jax.random.fold_in(key, 2)
    return drawn_draw(key).astype(jnp.bfloat16)


def draw_q_time(key, part):
    key = jax.random.fold_in(key, 3)
    return drawn_draw(key).astype(jnp.bfloat16)


def draw_k_time(key, part):
    key = jax.random.fold_in(key, 4)
    return drawn_draw(key).astype(jnp.bfloat16)


def shard_levels(stream_key, shape, pieces, least, largest):
    level, own = 1.0, jax.random.fold_in(stream_key, 6)
    for axis_at, shards_of in pieces:
        heights = jnp.exp(jax.random.uniform(jax.random.fold_in(own, axis_at), (shards_of,), jnp.float32, least / len(pieces), largest / len(pieces)))
        level = level * jnp.repeat(heights, shape[axis_at] // shards_of).reshape([-1 if axis == axis_at else 1 for axis in range(len(shape))])
    return level


def scatter_about(key, extent, spread, most, pieces=(), kind=jnp.bfloat16):
    factor_of = shard_levels(key, extent, pieces, -0.22, 0.18) if pieces else 1.0
    entries = jax.random.normal(key, extent, jnp.float32) * spread * factor_of
    return jnp.minimum(jnp.maximum(entries, -most), most).astype(kind)


def setup_inputs(seed: int = 0, part: int = 0) -> dict:
    seeds = jax.random.split(jax.random.key(seed), 7)
    part_keys = jax.random.split(jax.random.fold_in(seeds[6], part), 7)
    q_space = draw_q_space(jax.random.fold_in(jax.random.fold_in(seeds[6], part), 71), part)
    k_space = draw_k_space(jax.random.fold_in(jax.random.fold_in(seeds[6], part), 71), part)
    v_space = scatter_about(part_keys[2], (FRAMES, POS, HEADS * HEAD_DIM), 1.0, 6.0, ((0, 32),))
    q_time = draw_q_time(jax.random.fold_in(jax.random.fold_in(seeds[6], part), 71), part)
    k_time = draw_k_time(jax.random.fold_in(jax.random.fold_in(seeds[6], part), 71), part)
    grad_out = scatter_about(part_keys[5], (FRAMES, POS, HEADS * HEAD_DIM), 1.0, 6.0, ((0, 32),))
    return {"q_space": q_space, "k_space": k_space, "v_space": v_space, "q_time": q_time, "k_time": k_time, "grad_out": grad_out}


SPACE = ("bqhd", "bkhd", "bhqk")
TIME = ("qbhd", "kbhd", "bhqk")


def split_heads(tensor):
    return tensor.reshape(tensor.shape[:-1] + (HEADS, HEAD_DIM)).astype(jnp.float32)


def join_heads(tensor):
    return tensor.reshape(tensor.shape[:-2] + (HEADS * HEAD_DIM,)).astype(jnp.bfloat16)


def product(first_form, second_form, result_form, left, right):
    return jnp.einsum(first_form + "," + second_form + "->" + result_form, left, right)


def widened(tensor):
    return lax.optimization_barrier(tensor.astype(jnp.bfloat16)).astype(jnp.float32)


def probabilities(queries, key_rows, layout):
    scores = product(layout[0], layout[1], layout[2], queries, key_rows) * HEAD_DIM ** -0.5
    weights = jax.nn.softmax(scores, axis=-1)
    return weights, widened(weights)


def attend_backward(queries, key_rows, values, weights, rounded, upstream, layout):
    weight_grads = product(layout[0], layout[1], layout[2], upstream, values)
    value_grads = product(layout[2], layout[0], layout[1], rounded, upstream)
    score_grads = weights * (weight_grads - jnp.sum(weights * weight_grads, axis=-1, keepdims=True))
    score_grads = widened(score_grads)
    query_grads = product(layout[2], layout[1], layout[0], score_grads, key_rows) * HEAD_DIM ** -0.5
    key_grads = product(layout[2], layout[0], layout[1], score_grads, queries) * HEAD_DIM ** -0.5
    return query_grads, key_grads, value_grads


def space_forward(frame_data):
    queries, key_rows, values = [split_heads(part_one[None]) for part_one in frame_data]
    weights, rounded = probabilities(queries, key_rows, SPACE)
    output = product(SPACE[2], SPACE[1], SPACE[0], rounded, values)
    return join_heads(output)[0]


def space_backward(frame_data):
    queries, key_rows, values, upstream = [split_heads(part_one[None]) for part_one in frame_data]
    weights, rounded = probabilities(queries, key_rows, SPACE)
    grads = attend_backward(queries, key_rows, values, weights, rounded, upstream, SPACE)
    return tuple(join_heads(entry)[0] for entry in grads)


def reference(q_space, k_space, v_space, q_time, k_time, grad_out):
    space_out = lax.map(space_forward, (q_space, k_space, v_space))
    time_query = split_heads(q_time)
    time_keys = split_heads(k_time)
    time_values = split_heads(space_out)
    time_upstream = split_heads(grad_out)
    weights, rounded = probabilities(time_query, time_keys, TIME)
    query_grads, key_grads, value_grads = attend_backward(time_query, time_keys, time_values, weights, rounded, time_upstream, TIME)
    grad_space = join_heads(value_grads)
    grad_q_space, grad_k_space, grad_v_space = lax.map(space_backward, (q_space, k_space, v_space, grad_space))
    return (grad_q_space, grad_k_space, grad_v_space, join_heads(query_grads), join_heads(key_grads))
```

```python
import functools
import math

import jax
import jax.numpy as jnp
from jax import lax
from jax.experimental import pallas as pl
from jax.experimental.pallas import tpu as pltpu
from jax.sharding import PartitionSpec as P

HEADS = 16
HEAD_DIM = 128
SCALE = HEAD_DIM**-0.5
SCALE2 = SCALE * math.log2(math.e)
MESH = pl.DeviceIdType.MESH

FRAMES = 32
POS = 512
OWN = POS // FRAMES
WIDTH = HEADS * HEAD_DIM
CHUNKS = 4
COLS = WIDTH // CHUNKS
CHUNK_HEADS = HEADS // CHUNKS


def product(left, right, contract):
    return lax.dot_general(left, right, (contract, ((), ())), preferred_element_type=jnp.float32)


def plain(left, right):
    return product(left, right, ((1,), (0,)))


def against(left, right):
    return product(left, right, ((1,), (1,)))


def probabilities(queries, key_rows, bias=None):
    scores = against(key_rows, queries) * SCALE2
    if bias is not None:
        scores = (scores.reshape(FRAMES, OWN, POS) + bias[None]).reshape(POS, POS)
    scores = jnp.exp2(scores - jnp.max(scores, axis=0, keepdims=True))
    return scores * (1.0 / jnp.sum(scores, axis=0, keepdims=True))


def backward(queries, key_rows, values, upstream, bias=None):
    weights = probabilities(queries, key_rows, bias)
    value_grads = plain(weights.astype(jnp.bfloat16), upstream)
    weight_grads = against(values, upstream)
    weighted = weights * weight_grads
    score_grads = weighted - weights * jnp.sum(weighted, axis=0, keepdims=True)
    score_grads = score_grads.astype(jnp.bfloat16)
    key_grads = plain(score_grads, queries) * SCALE
    query_grads = (plain(key_rows.T, score_grads) * SCALE).T
    return (
        query_grads.astype(jnp.bfloat16),
        key_grads.astype(jnp.bfloat16),
        value_grads.astype(jnp.bfloat16),
    )


def kernel(
    q_space, k_space, v_space, q_time, k_time, grad_out,
    gq_space, gk_space, gv_space, gq_time, gk_time,
    sq, sk, sv, so, gs, held, made, done, bias,
    load_sem, send_sem, qkg_sem, so_sem, gs_sem, back_sem, own_sem, store_sem,
):
    seq, dp = lax.axis_index("seq"), lax.axis_index("dp")
    my_rows = pl.ds(pl.multiple_of(seq * OWN, OWN), OWN)

    def columns(chunk):
        return pl.ds(pl.multiple_of(chunk * COLS, COLS), COLS)

    def head_columns(head):
        return pl.ds(pl.multiple_of(head * HEAD_DIM, HEAD_DIM), HEAD_DIM)

    def peer_of(step):
        y = lax.rem(seq // 8 + step // 8, 4)
        z = lax.rem(seq // 4 + step // 4, 2)
        x = lax.rem(seq + step, 4)
        return y * 8 + z * 4 + x

    def rows_of(device):
        return pl.ds(pl.multiple_of(device * OWN, OWN), OWN)

    def spread(chunk, moves):
        cols = columns(chunk)

        def one(step, carry):
            peer = peer_of(step)
            for source, target, sent, landed in moves:
                pltpu.make_async_remote_copy(
                    src_ref=source.at[rows_of(peer), cols],
                    dst_ref=target.at[my_rows, cols],
                    send_sem=sent,
                    recv_sem=landed,
                    device_id=(dp, peer),
                    device_id_type=MESH,
                ).start()
            return carry

        lax.fori_loop(1, FRAMES, one, 0)
        for source, target, sent, landed in moves:
            pltpu.make_async_copy(
                source.at[my_rows, cols], target.at[my_rows, cols], landed
            ).start()

    def wait_for(ref, sem):
        pltpu.make_async_copy(ref, ref, sem).wait()

    spatial = ((q_space, sq), (k_space, sk), (v_space, sv))
    for chunk in range(CHUNKS):
        cols = pl.ds(chunk * COLS, COLS)
        for at, (source, target) in enumerate(spatial):
            pltpu.make_async_copy(
                source.at[:, cols], target.at[:, cols], load_sem.at[at, chunk]
            ).start()

    def send_inputs(chunk, carry):
        spread(
            chunk,
            [
                (source, held.at[at], send_sem.at[at], qkg_sem.at[at, chunk])
                for at, source in enumerate((q_time, k_time, grad_out))
            ],
        )
        return carry

    lax.fori_loop(0, CHUNKS, send_inputs, 0)

    rows = lax.broadcasted_iota(jnp.int32, (OWN, POS), 0)
    lanes = lax.broadcasted_iota(jnp.int32, (OWN, POS), 1)
    bias[...] = jnp.where(rows == lanes % OWN, 0.0, -1e30).astype(jnp.float32)

    def space_forward(chunk, carry):
        cols = columns(chunk)
        for at, (source, target) in enumerate(spatial):
            wait_for(target.at[:, cols], load_sem.at[at, chunk])

        def one(index, carry):
            here = head_columns(chunk * CHUNK_HEADS + index)
            weights = probabilities(sq[:, here], sk[:, here]).astype(jnp.bfloat16)
            so[:, here] = plain(sv[:, here].T, weights).T.astype(jnp.bfloat16)
            return carry

        lax.fori_loop(0, CHUNK_HEADS, one, 0)
        spread(chunk, [(so, held.at[3], send_sem.at[3], so_sem.at[chunk])])
        return carry

    lax.fori_loop(0, CHUNKS, space_forward, 0)

    def time_core(chunk, carry):
        cols = columns(chunk)
        for at in range(3):
            wait_for(held.at[at, :, cols], qkg_sem.at[at, chunk])
        wait_for(held.at[3, :, cols], so_sem.at[chunk])

        def one(index, carry):
            here = head_columns(chunk * CHUNK_HEADS + index)
            query_grads, key_grads, value_grads = backward(
                held[0, :, here], held[1, :, here], held[3, :, here], held[2, :, here], bias[...]
            )
            made[0, :, here] = value_grads
            made[1, :, here] = query_grads
            made[2, :, here] = key_grads
            return carry

        lax.fori_loop(0, CHUNK_HEADS, one, 0)
        spread(chunk, [(made.at[0], gs, send_sem.at[4], gs_sem.at[chunk])])
        spread(
            chunk,
            [
                (made.at[1], gq_time, send_sem.at[5], back_sem.at[0]),
                (made.at[2], gk_time, send_sem.at[6], back_sem.at[1]),
            ],
        )
        return carry

    lax.fori_loop(0, CHUNKS, time_core, 0)

    outs = (gq_space, gk_space, gv_space)

    def space_back(chunk, carry):
        cols = columns(chunk)
        wait_for(gs.at[:, cols], gs_sem.at[chunk])

        def one(index, carry):
            here = head_columns(chunk * CHUNK_HEADS + index)
            grads = backward(sq[:, here], sk[:, here], sv[:, here], gs[:, here])
            for at in range(3):
                done[at, :, here] = grads[at]
            return carry

        lax.fori_loop(0, CHUNK_HEADS, one, 0)
        for at in range(3):
            pltpu.make_async_copy(
                done.at[at, :, cols], outs[at].at[:, cols], store_sem.at[at, chunk]
            ).start()
        return carry

    lax.fori_loop(0, CHUNKS, space_back, 0)

    sent = POS - OWN
    for at in range(7):
        wait_for(held.at[0, pl.ds(0, sent)], send_sem.at[at])
    wait_for(gq_time, back_sem.at[0])
    wait_for(gk_time, back_sem.at[1])

    def stored(chunk, carry):
        for at in range(3):
            pltpu.make_async_copy(
                done.at[at, :, columns(chunk)],
                outs[at].at[:, columns(chunk)],
                store_sem.at[at, chunk],
            ).wait()
        return carry

    lax.fori_loop(0, CHUNKS, stored, 0)


def shards(*arrays):
    array = pl.BlockSpec(memory_space=pl.ANY)
    whole = pltpu.VMEM((POS, WIDTH), jnp.bfloat16)
    dma = pltpu.SemaphoreType.DMA
    products = 12 * 2 * HEADS * POS * POS * HEAD_DIM
    grads = pl.pallas_call(
        kernel,
        out_shape=[jax.ShapeDtypeStruct((POS, WIDTH), jnp.bfloat16)] * 5,
        in_specs=[array] * 6,
        out_specs=[array] * 5,
        scratch_shapes=[
            whole, whole, whole, whole, whole,
            pltpu.VMEM((4, POS, WIDTH), jnp.bfloat16),
            pltpu.VMEM((3, POS, WIDTH), jnp.bfloat16),
            pltpu.VMEM((3, POS, WIDTH), jnp.bfloat16),
            pltpu.VMEM((OWN, POS), jnp.float32),
            dma((3, CHUNKS)), dma((7,)), dma((3, CHUNKS)), dma((CHUNKS,)), dma((CHUNKS,)),
            dma((2,)), dma((1,)), dma((3, CHUNKS)),
        ],
        compiler_params=pltpu.CompilerParams(has_side_effects=True, vmem_limit_bytes=60 << 20),
        cost_estimate=pl.CostEstimate(
            flops=products,
            bytes_accessed=22 * POS * WIDTH,
            transcendentals=3 * HEADS * POS * POS,
        ),
        name="attention",
    )(*(array.reshape(POS, WIDTH) for array in arrays))
    return tuple(entry[None] for entry in grads)


def solution(mesh):
    spec = P(("dp", "seq"), None, None)
    return jax.shard_map(
        shards, mesh=mesh, in_specs=(spec,) * 6, out_specs=(spec,) * 5, check_vma=False
    )
```

```python
import functools
import math

import jax
import jax.numpy as jnp
from jax import lax
from jax.experimental import pallas as pl
from jax.experimental.pallas import tpu as pltpu
from jax.sharding import PartitionSpec as P

HEADS = 16
HEAD_DIM = 128
SCALE = HEAD_DIM**-0.5
SCALE2 = SCALE * math.log2(math.e)
MESH = pl.DeviceIdType.MESH

FRAMES = 32
POS = 512
OWN = POS // FRAMES
WIDTH = HEADS * HEAD_DIM
CHUNKS = 4
COLS = WIDTH // CHUNKS
CHUNK_HEADS = HEADS // CHUNKS


def product(left, right, contract):
    return lax.dot_general(left, right, (contract, ((), ())), preferred_element_type=jnp.float32)


def plain(left, right):
    return product(left, right, ((1,), (0,)))


def against(left, right):
    return product(left, right, ((1,), (1,)))


def probabilities(queries, key_rows, bias=None):
    scores = against(key_rows, queries) * SCALE2
    if bias is not None:
        scores = (scores.reshape(FRAMES, OWN, POS) + bias[None]).reshape(POS, POS)
    scores = jnp.exp2(scores - jnp.max(scores, axis=0, keepdims=True))
    return scores * (1.0 / jnp.sum(scores, axis=0, keepdims=True))


def score_backward(queries, key_rows, values, weights, upstream):
    weight_grads = against(values, upstream)
    weighted = weights * weight_grads
    score_grads = weighted - weights * jnp.sum(weighted, axis=0, keepdims=True)
    score_grads = score_grads.astype(jnp.bfloat16)
    key_grads = plain(score_grads, queries) * SCALE
    query_grads = (plain(key_rows.T, score_grads) * SCALE).T
    return query_grads.astype(jnp.bfloat16), key_grads.astype(jnp.bfloat16)


def value_backward(weights, upstream):
    return plain(weights.astype(jnp.bfloat16), upstream).astype(jnp.bfloat16)


def kernel(
    q_space, k_space, v_space, q_time, k_time, grad_out,
    gq_space, gk_space, gv_space, gq_time, gk_time,
    sq, sk, sv, so, gs, held, made, bias,
    load_sem, send_sem, qkg_sem, so_sem, gs_sem, back_sem,
):
    seq, dp = lax.axis_index("seq"), lax.axis_index("dp")
    my_rows = pl.ds(pl.multiple_of(seq * OWN, OWN), OWN)

    def columns(chunk):
        return pl.ds(pl.multiple_of(chunk * COLS, COLS), COLS)

    def head_columns(head):
        return pl.ds(pl.multiple_of(head * HEAD_DIM, HEAD_DIM), HEAD_DIM)

    def peer_of(step):
        y = lax.rem(seq // 8 + step // 8, 4)
        z = lax.rem(seq // 4 + step // 4, 2)
        x = lax.rem(seq + step, 4)
        return y * 8 + z * 4 + x

    def rows_of(device):
        return pl.ds(pl.multiple_of(device * OWN, OWN), OWN)

    def spread(chunk, moves):
        cols = columns(chunk)

        def one(step, carry):
            peer = peer_of(step)
            for source, target, sent, landed in moves:
                pltpu.make_async_remote_copy(
                    src_ref=source.at[rows_of(peer), cols],
                    dst_ref=target.at[my_rows, cols],
                    send_sem=sent,
                    recv_sem=landed,
                    device_id=(dp, peer),
                    device_id_type=MESH,
                ).start()
            return carry

        lax.fori_loop(1, FRAMES, one, 0)
        for source, target, sent, landed in moves:
            pltpu.make_async_copy(
                source.at[my_rows, cols], target.at[my_rows, cols], landed
            ).start()

    def wait_for(ref, sem):
        pltpu.make_async_copy(ref, ref, sem).wait()

    spatial = ((q_space, sq), (k_space, sk), (v_space, sv))
    for chunk in range(CHUNKS):
        cols = pl.ds(chunk * COLS, COLS)
        for at, (source, target) in enumerate(spatial):
            pltpu.make_async_copy(
                source.at[:, cols], target.at[:, cols], load_sem.at[at, chunk]
            ).start()

    def send_inputs(chunk, carry):
        spread(
            chunk,
            [
                (source, held.at[at], send_sem.at[at], qkg_sem.at[at, chunk])
                for at, source in enumerate((q_time, k_time, grad_out))
            ],
        )
        return carry

    lax.fori_loop(0, CHUNKS, send_inputs, 0)

    rows = lax.broadcasted_iota(jnp.int32, (OWN, POS), 0)
    lanes = lax.broadcasted_iota(jnp.int32, (OWN, POS), 1)
    bias[...] = jnp.where(rows == lanes % OWN, 0.0, -1e30).astype(jnp.float32)

    def space_forward(chunk, carry):
        cols = columns(chunk)
        for at, (source, target) in enumerate(spatial):
            wait_for(target.at[:, cols], load_sem.at[at, chunk])

        def one(index, carry):
            here = head_columns(chunk * CHUNK_HEADS + index)
            weights = probabilities(sq[:, here], sk[:, here]).astype(jnp.bfloat16)
            so[:, here] = plain(sv[:, here].T, weights).T.astype(jnp.bfloat16)
            return carry

        lax.fori_loop(0, CHUNK_HEADS, one, 0)
        spread(chunk, [(so, held.at[3], send_sem.at[3], so_sem.at[chunk])])
        return carry

    lax.fori_loop(0, CHUNKS, space_forward, 0)

    def each_head(chunk, work):
        def one(index, carry):
            work(head_columns(chunk * CHUNK_HEADS + index))
            return carry

        lax.fori_loop(0, CHUNK_HEADS, one, 0)

    def time_weights(here):
        return probabilities(held[0, :, here], held[1, :, here], bias[...])

    def time_values(chunk, carry):
        cols = columns(chunk)
        for at in range(3):
            wait_for(held.at[at, :, cols], qkg_sem.at[at, chunk])

        def work(here):
            made[0, :, here] = value_backward(time_weights(here), held[2, :, here])

        each_head(chunk, work)
        spread(chunk, [(made.at[0], gs, send_sem.at[4], gs_sem.at[chunk])])
        return carry

    lax.fori_loop(0, CHUNKS, time_values, 0)

    def time_scores(chunk, carry):
        wait_for(held.at[3, :, columns(chunk)], so_sem.at[chunk])

        def work(here):
            made[1, :, here], made[2, :, here] = score_backward(
                held[0, :, here], held[1, :, here], held[3, :, here], time_weights(here), held[2, :, here]
            )

        each_head(chunk, work)
        spread(
            chunk,
            [
                (made.at[1], gq_time, send_sem.at[5], back_sem.at[0]),
                (made.at[2], gk_time, send_sem.at[6], back_sem.at[1]),
            ],
        )
        return carry

    lax.fori_loop(0, CHUNKS, time_scores, 0)

    def space_back(chunk, carry):
        wait_for(gs.at[:, columns(chunk)], gs_sem.at[chunk])

        def work(here):
            weights = probabilities(sq[:, here], sk[:, here])
            gv_space[:, here] = value_backward(weights, gs[:, here])
            gq_space[:, here], gk_space[:, here] = score_backward(
                sq[:, here], sk[:, here], sv[:, here], weights, gs[:, here]
            )

        each_head(chunk, work)
        return carry

    lax.fori_loop(0, CHUNKS, space_back, 0)

    sent = POS - OWN
    for at in range(7):
        wait_for(held.at[0, pl.ds(0, sent)], send_sem.at[at])
    wait_for(gq_time, back_sem.at[0])
    wait_for(gk_time, back_sem.at[1])


def write_out(*refs):
    sources, targets, sem = refs[:5], refs[5:10], refs[10]
    copies = [
        pltpu.make_async_copy(source, target, sem.at[at])
        for at, (source, target) in enumerate(zip(sources, targets))
    ]
    for copy in copies:
        copy.start()
    for copy in copies:
        copy.wait()


def shards(*arrays):
    array = pl.BlockSpec(memory_space=pl.ANY)
    whole = pltpu.VMEM((POS, WIDTH), jnp.bfloat16)
    dma = pltpu.SemaphoreType.DMA
    products = 12 * 2 * HEADS * POS * POS * HEAD_DIM
    grads = pl.pallas_call(
        kernel,
        out_shape=[pltpu.VMEM((POS, WIDTH), jnp.bfloat16)] * 5,
        in_specs=[array] * 6,
        out_specs=[pl.BlockSpec(memory_space=pltpu.VMEM)] * 5,
        scratch_shapes=[
            whole, whole, whole, whole, whole,
            pltpu.VMEM((4, POS, WIDTH), jnp.bfloat16),
            pltpu.VMEM((3, POS, WIDTH), jnp.bfloat16),
            pltpu.VMEM((OWN, POS), jnp.float32),
            dma((3, CHUNKS)), dma((7,)), dma((3, CHUNKS)), dma((CHUNKS,)), dma((CHUNKS,)), dma((2,)),
        ],
        compiler_params=pltpu.CompilerParams(has_side_effects=True, vmem_limit_bytes=46 << 20),
        cost_estimate=pl.CostEstimate(
            flops=products,
            bytes_accessed=12 * POS * WIDTH,
            transcendentals=4 * HEADS * POS * POS,
        ),
        name="attention",
    )(*(array.reshape(POS, WIDTH) for array in arrays))
    grads = pl.pallas_call(
        write_out,
        out_shape=[jax.ShapeDtypeStruct((POS, WIDTH), jnp.bfloat16)] * 5,
        in_specs=[array] * 5,
        out_specs=[array] * 5,
        scratch_shapes=[dma((5,))],
        compiler_params=pltpu.CompilerParams(vmem_limit_bytes=1 << 20),
        cost_estimate=pl.CostEstimate(
            flops=0, bytes_accessed=20 * POS * WIDTH, transcendentals=0
        ),
        name="write_out",
    )(*grads)
    return tuple(entry[None] for entry in grads)


def solution(mesh):
    spec = P(("dp", "seq"), None, None)
    return jax.shard_map(
        shards, mesh=mesh, in_specs=(spec,) * 6, out_specs=(spec,) * 5, check_vma=False
    )
```

```python
import functools
import math

import jax
import jax.numpy as jnp
from jax import lax
from jax.experimental import pallas as pl
from jax.experimental.pallas import tpu as pltpu
from jax.sharding import PartitionSpec as P

HEADS = 16
HEAD_DIM = 128
SCALE = HEAD_DIM**-0.5
SCALE2 = SCALE * math.log2(math.e)
MESH = pl.DeviceIdType.MESH

FRAMES = 32
POS = 512
OWN = POS // FRAMES
WIDTH = HEADS * HEAD_DIM
CHUNKS = 8
COLS = WIDTH // CHUNKS
CHUNK_HEADS = HEADS // CHUNKS


def product(left, right, contract):
    return lax.dot_general(left, right, (contract, ((), ())), preferred_element_type=jnp.float32)


def plain(left, right):
    return product(left, right, ((1,), (0,)))


def against(left, right):
    return product(left, right, ((1,), (1,)))


def probabilities(queries, key_rows, bias=None):
    scores = against(key_rows, queries) * SCALE2
    if bias is not None:
        scores = (scores.reshape(FRAMES, OWN, POS) + bias[None]).reshape(POS, POS)
    scores = jnp.exp2(scores - jnp.max(scores, axis=0, keepdims=True))
    return scores * (1.0 / jnp.sum(scores, axis=0, keepdims=True))


def score_backward(queries, key_rows, values, weights, upstream):
    weight_grads = against(values, upstream)
    weighted = weights * weight_grads
    score_grads = weighted - weights * jnp.sum(weighted, axis=0, keepdims=True)
    score_grads = score_grads.astype(jnp.bfloat16)
    key_grads = plain(score_grads, queries) * SCALE
    query_grads = (plain(key_rows.T, score_grads) * SCALE).T
    return query_grads.astype(jnp.bfloat16), key_grads.astype(jnp.bfloat16)


def value_backward(weights, upstream):
    return plain(weights.astype(jnp.bfloat16), upstream).astype(jnp.bfloat16)


def kernel(
    q_space, k_space, v_space, q_time, k_time, grad_out,
    gq_space, gk_space, gv_space, gq_time, gk_time,
    sq, sk, sv, so, gs, held, made, bias,
    load_sem, send_sem, qkg_sem, so_sem, gs_sem, back_sem,
):
    seq, dp = lax.axis_index("seq"), lax.axis_index("dp")
    my_rows = pl.ds(pl.multiple_of(seq * OWN, OWN), OWN)

    def columns(chunk):
        return pl.ds(pl.multiple_of(chunk * COLS, COLS), COLS)

    def head_columns(head):
        return pl.ds(pl.multiple_of(head * HEAD_DIM, HEAD_DIM), HEAD_DIM)

    def peer_of(step):
        y = lax.rem(seq // 8 + step // 8, 4)
        z = lax.rem(seq // 4 + step // 4, 2)
        x = lax.rem(seq + step, 4)
        return y * 8 + z * 4 + x

    def rows_of(device):
        return pl.ds(pl.multiple_of(device * OWN, OWN), OWN)

    def spread(chunk, source, target, sent, landed):
        cols = columns(chunk)

        def one(step, carry):
            peer = peer_of(step)
            pltpu.make_async_remote_copy(
                src_ref=source.at[rows_of(peer), cols],
                dst_ref=target.at[my_rows, cols],
                send_sem=sent,
                recv_sem=landed,
                device_id=(dp, peer),
                device_id_type=MESH,
            ).start()
            return carry

        lax.fori_loop(1, FRAMES, one, 0)
        pltpu.make_async_copy(source.at[my_rows, cols], target.at[my_rows, cols], landed).start()

    def wait_for(ref, sem):
        pltpu.make_async_copy(ref, ref, sem).wait()

    spatial = ((q_space, sq), (k_space, sk), (v_space, sv))
    for chunk in range(CHUNKS):
        cols = pl.ds(chunk * COLS, COLS)
        for at, (source, target) in enumerate(spatial):
            pltpu.make_async_copy(
                source.at[:, cols], target.at[:, cols], load_sem.at[at, chunk]
            ).start()

    def send_inputs(chunk, carry):
        for at, source in enumerate((q_time, k_time, grad_out)):
            spread(chunk, source, held.at[at], send_sem.at[at], qkg_sem.at[at, chunk])
        return carry

    lax.fori_loop(0, CHUNKS, send_inputs, 0)

    rows = lax.broadcasted_iota(jnp.int32, (OWN, POS), 0)
    lanes = lax.broadcasted_iota(jnp.int32, (OWN, POS), 1)
    bias[...] = jnp.where(rows == lanes % OWN, 0.0, -1e30).astype(jnp.float32)

    def space_forward(chunk, carry):
        cols = columns(chunk)
        for at, (source, target) in enumerate(spatial):
            wait_for(target.at[:, cols], load_sem.at[at, chunk])

        def one(index, carry):
            here = head_columns(chunk * CHUNK_HEADS + index)
            weights = probabilities(sq[:, here], sk[:, here]).astype(jnp.bfloat16)
            so[:, here] = plain(sv[:, here].T, weights).T.astype(jnp.bfloat16)
            return carry

        lax.fori_loop(0, CHUNK_HEADS, one, 0)
        spread(chunk, so, held.at[3], send_sem.at[3], so_sem.at[chunk])
        return carry

    lax.fori_loop(0, CHUNKS, space_forward, 0)

    def each_head(chunk, work):
        def one(index, carry):
            work(head_columns(chunk * CHUNK_HEADS + index))
            return carry

        lax.fori_loop(0, CHUNK_HEADS, one, 0)

    def time_weights(here):
        return probabilities(held[0, :, here], held[1, :, here], bias[...])

    def time_values(chunk, carry):
        cols = columns(chunk)
        for at in range(3):
            wait_for(held.at[at, :, cols], qkg_sem.at[at, chunk])

        def work(here):
            made[0, :, here] = value_backward(time_weights(here), held[2, :, here])

        each_head(chunk, work)
        spread(chunk, made.at[0], gs, send_sem.at[4], gs_sem.at[chunk])
        return carry

    lax.fori_loop(0, CHUNKS, time_values, 0)

    def time_scores(chunk, carry):
        wait_for(held.at[3, :, columns(chunk)], so_sem.at[chunk])

        def work(here):
            made[1, :, here], made[2, :, here] = score_backward(
                held[0, :, here], held[1, :, here], held[3, :, here], time_weights(here), held[2, :, here]
            )

        each_head(chunk, work)
        spread(chunk, made.at[1], gq_time, send_sem.at[5], back_sem.at[0])
        spread(chunk, made.at[2], gk_time, send_sem.at[6], back_sem.at[1])
        return carry

    lax.fori_loop(0, CHUNKS, time_scores, 0)

    def space_back(chunk, carry):
        wait_for(gs.at[:, columns(chunk)], gs_sem.at[chunk])

        def work(here):
            weights = probabilities(sq[:, here], sk[:, here])
            gv_space[:, here] = value_backward(weights, gs[:, here])
            gq_space[:, here], gk_space[:, here] = score_backward(
                sq[:, here], sk[:, here], sv[:, here], weights, gs[:, here]
            )

        each_head(chunk, work)
        return carry

    lax.fori_loop(0, CHUNKS, space_back, 0)

    sent = POS - OWN
    for at in range(7):
        wait_for(held.at[0, pl.ds(0, sent)], send_sem.at[at])
    wait_for(gq_time, back_sem.at[0])
    wait_for(gk_time, back_sem.at[1])


def write_out(*refs):
    sources, targets, sem = refs[:5], refs[5:10], refs[10]
    copies = [
        pltpu.make_async_copy(source, target, sem.at[at])
        for at, (source, target) in enumerate(zip(sources, targets))
    ]
    for copy in copies:
        copy.start()
    for copy in copies:
        copy.wait()


def shards(*arrays):
    array = pl.BlockSpec(memory_space=pl.ANY)
    whole = pltpu.VMEM((POS, WIDTH), jnp.bfloat16)
    dma = pltpu.SemaphoreType.DMA
    products = 12 * 2 * HEADS * POS * POS * HEAD_DIM
    grads = pl.pallas_call(
        kernel,
        out_shape=[pltpu.VMEM((POS, WIDTH), jnp.bfloat16)] * 5,
        in_specs=[array] * 6,
        out_specs=[pl.BlockSpec(memory_space=pltpu.VMEM)] * 5,
        scratch_shapes=[
            whole, whole, whole, whole, whole,
            pltpu.VMEM((4, POS, WIDTH), jnp.bfloat16),
            pltpu.VMEM((3, POS, WIDTH), jnp.bfloat16),
            pltpu.VMEM((OWN, POS), jnp.float32),
            dma((3, CHUNKS)), dma((7,)), dma((3, CHUNKS)), dma((CHUNKS,)), dma((CHUNKS,)), dma((2,)),
        ],
        compiler_params=pltpu.CompilerParams(has_side_effects=True, vmem_limit_bytes=46 << 20),
        cost_estimate=pl.CostEstimate(
            flops=products,
            bytes_accessed=12 * POS * WIDTH,
            transcendentals=4 * HEADS * POS * POS,
        ),
        name="attention",
    )(*(array.reshape(POS, WIDTH) for array in arrays))
    grads = pl.pallas_call(
        write_out,
        out_shape=[jax.ShapeDtypeStruct((POS, WIDTH), jnp.bfloat16)] * 5,
        in_specs=[array] * 5,
        out_specs=[array] * 5,
        scratch_shapes=[dma((5,))],
        compiler_params=pltpu.CompilerParams(vmem_limit_bytes=1 << 20),
        cost_estimate=pl.CostEstimate(
            flops=0, bytes_accessed=20 * POS * WIDTH, transcendentals=0
        ),
        name="write_out",
    )(*grads)
    return tuple(entry[None] for entry in grads)


def solution(mesh):
    spec = P(("dp", "seq"), None, None)
    return jax.shard_map(
        shards, mesh=mesh, in_specs=(spec,) * 6, out_specs=(spec,) * 5, check_vma=False
    )
```

```python
import functools
import math

import jax
import jax.numpy as jnp
from jax import lax
from jax.experimental import pallas as pl
from jax.experimental.pallas import tpu as pltpu
from jax.sharding import PartitionSpec as P

HEADS = 16
HEAD_DIM = 128
SCALE = HEAD_DIM**-0.5
SCALE2 = SCALE * math.log2(math.e)
MESH = pl.DeviceIdType.MESH

FRAMES = 32
POS = 512
OWN = POS // FRAMES
WIDTH = HEADS * HEAD_DIM
CHUNKS = 8
COLS = WIDTH // CHUNKS
CHUNK_HEADS = HEADS // CHUNKS


def product(left, right, contract):
    return lax.dot_general(left, right, (contract, ((), ())), preferred_element_type=jnp.float32)


def plain(left, right):
    return product(left, right, ((1,), (0,)))


def against(left, right):
    return product(left, right, ((1,), (1,)))


def probabilities(queries, key_rows, bias=None):
    scores = against(key_rows, queries) * SCALE2
    if bias is not None:
        scores = (scores.reshape(FRAMES, OWN, POS) + bias[None]).reshape(POS, POS)
    scores = jnp.exp2(scores - jnp.max(scores, axis=0, keepdims=True))
    return scores * (1.0 / jnp.sum(scores, axis=0, keepdims=True))


def score_backward(queries, key_rows, values, weights, upstream):
    weight_grads = against(values, upstream)
    weighted = weights * weight_grads
    score_grads = weighted - weights * jnp.sum(weighted, axis=0, keepdims=True)
    score_grads = score_grads.astype(jnp.bfloat16)
    key_grads = plain(score_grads, queries) * SCALE
    query_grads = (plain(key_rows.T, score_grads) * SCALE).T
    return query_grads.astype(jnp.bfloat16), key_grads.astype(jnp.bfloat16)


def value_backward(weights, upstream):
    return plain(weights.astype(jnp.bfloat16), upstream).astype(jnp.bfloat16)


def kernel(
    q_space, k_space, v_space, q_time, k_time, grad_out,
    gq_space, gk_space, gv_space, gq_time, gk_time,
    sq, sk, sv, so, gs, held, made, bias,
    load_sem, send_sem, qkg_sem, so_sem, gs_sem, back_sem,
):
    seq, dp = lax.axis_index("seq"), lax.axis_index("dp")
    my_rows = pl.ds(pl.multiple_of(seq * OWN, OWN), OWN)

    def columns(chunk):
        return pl.ds(pl.multiple_of(chunk * COLS, COLS), COLS)

    def head_columns(head):
        return pl.ds(pl.multiple_of(head * HEAD_DIM, HEAD_DIM), HEAD_DIM)

    def peer_of(step):
        y = lax.rem(seq // 8 + step // 8, 4)
        z = lax.rem(seq // 4 + step // 4, 2)
        x = lax.rem(seq + step, 4)
        return y * 8 + z * 4 + x

    def rows_of(device):
        return pl.ds(pl.multiple_of(device * OWN, OWN), OWN)

    def spread(chunk, source, target, sent, landed):
        cols = columns(chunk)

        def one(step, carry):
            peer = peer_of(step)
            pltpu.make_async_remote_copy(
                src_ref=source.at[rows_of(peer), cols],
                dst_ref=target.at[my_rows, cols],
                send_sem=sent,
                recv_sem=landed,
                device_id=(dp, peer),
                device_id_type=MESH,
            ).start()
            return carry

        lax.fori_loop(1, FRAMES, one, 0)
        pltpu.make_async_copy(source.at[my_rows, cols], target.at[my_rows, cols], landed).start()

    def wait_for(ref, sem):
        pltpu.make_async_copy(ref, ref, sem).wait()

    barrier = pltpu.get_barrier_semaphore()

    def greet(step, carry):
        pl.semaphore_signal(barrier, inc=1, device_id=(dp, peer_of(step)), device_id_type=MESH)
        return carry

    lax.fori_loop(1, FRAMES, greet, 0)
    pl.semaphore_wait(barrier, FRAMES - 1)

    spatial = ((q_space, sq), (k_space, sk), (v_space, sv))
    for chunk in range(CHUNKS):
        cols = pl.ds(chunk * COLS, COLS)
        for at, (source, target) in enumerate(spatial):
            pltpu.make_async_copy(
                source.at[:, cols], target.at[:, cols], load_sem.at[at, chunk]
            ).start()

    def send_inputs(chunk, carry):
        for at, source in enumerate((q_time, k_time, grad_out)):
            spread(chunk, source, held.at[at], send_sem.at[at], qkg_sem.at[at, chunk])
        return carry

    lax.fori_loop(0, CHUNKS, send_inputs, 0)

    rows = lax.broadcasted_iota(jnp.int32, (OWN, POS), 0)
    lanes = lax.broadcasted_iota(jnp.int32, (OWN, POS), 1)
    bias[...] = jnp.where(rows == lanes % OWN, 0.0, -1e30).astype(jnp.float32)

    def space_forward(chunk, carry):
        cols = columns(chunk)
        for at, (source, target) in enumerate(spatial):
            wait_for(target.at[:, cols], load_sem.at[at, chunk])

        def one(index, carry):
            here = head_columns(chunk * CHUNK_HEADS + index)
            weights = probabilities(sq[:, here], sk[:, here]).astype(jnp.bfloat16)
            so[:, here] = plain(sv[:, here].T, weights).T.astype(jnp.bfloat16)
            return carry

        lax.fori_loop(0, CHUNK_HEADS, one, 0)
        spread(chunk, so, held.at[3], send_sem.at[3], so_sem.at[chunk])
        return carry

    lax.fori_loop(0, CHUNKS, space_forward, 0)

    def each_head(chunk, work):
        def one(index, carry):
            work(head_columns(chunk * CHUNK_HEADS + index))
            return carry

        lax.fori_loop(0, CHUNK_HEADS, one, 0)

    def time_weights(here):
        return probabilities(held[0, :, here], held[1, :, here], bias[...])

    def time_values(chunk, carry):
        cols = columns(chunk)
        for at in range(3):
            wait_for(held.at[at, :, cols], qkg_sem.at[at, chunk])

        def work(here):
            made[0, :, here] = value_backward(time_weights(here), held[2, :, here])

        each_head(chunk, work)
        spread(chunk, made.at[0], gs, send_sem.at[4], gs_sem.at[chunk])
        return carry

    lax.fori_loop(0, CHUNKS, time_values, 0)

    def time_scores(chunk, carry):
        wait_for(held.at[3, :, columns(chunk)], so_sem.at[chunk])

        def work(here):
            made[1, :, here], made[2, :, here] = score_backward(
                held[0, :, here], held[1, :, here], held[3, :, here], time_weights(here), held[2, :, here]
            )

        each_head(chunk, work)
        spread(chunk, made.at[1], gq_time, send_sem.at[5], back_sem.at[0])
        spread(chunk, made.at[2], gk_time, send_sem.at[6], back_sem.at[1])
        return carry

    lax.fori_loop(0, CHUNKS, time_scores, 0)

    def space_back(chunk, carry):
        wait_for(gs.at[:, columns(chunk)], gs_sem.at[chunk])

        def work(here):
            weights = probabilities(sq[:, here], sk[:, here])
            gv_space[:, here] = value_backward(weights, gs[:, here])
            gq_space[:, here], gk_space[:, here] = score_backward(
                sq[:, here], sk[:, here], sv[:, here], weights, gs[:, here]
            )

        each_head(chunk, work)
        return carry

    lax.fori_loop(0, CHUNKS, space_back, 0)

    sent = POS - OWN
    for at in range(7):
        wait_for(held.at[0, pl.ds(0, sent)], send_sem.at[at])
    wait_for(gq_time, back_sem.at[0])
    wait_for(gk_time, back_sem.at[1])


def write_out(*refs):
    sources, targets, sem = refs[:5], refs[5:10], refs[10]
    copies = [
        pltpu.make_async_copy(source, target, sem.at[at])
        for at, (source, target) in enumerate(zip(sources, targets))
    ]
    for copy in copies:
        copy.start()
    for copy in copies:
        copy.wait()


def shards(*arrays):
    array = pl.BlockSpec(memory_space=pl.ANY)
    whole = pltpu.VMEM((POS, WIDTH), jnp.bfloat16)
    dma = pltpu.SemaphoreType.DMA
    products = 12 * 2 * HEADS * POS * POS * HEAD_DIM
    grads = pl.pallas_call(
        kernel,
        out_shape=[pltpu.VMEM((POS, WIDTH), jnp.bfloat16)] * 5,
        in_specs=[array] * 6,
        out_specs=[pl.BlockSpec(memory_space=pltpu.VMEM)] * 5,
        scratch_shapes=[
            whole, whole, whole, whole, whole,
            pltpu.VMEM((4, POS, WIDTH), jnp.bfloat16),
            pltpu.VMEM((3, POS, WIDTH), jnp.bfloat16),
            pltpu.VMEM((OWN, POS), jnp.float32),
            dma((3, CHUNKS)), dma((7,)), dma((3, CHUNKS)), dma((CHUNKS,)), dma((CHUNKS,)), dma((2,)),
        ],
        compiler_params=pltpu.CompilerParams(collective_id=0, has_side_effects=True, vmem_limit_bytes=46 << 20),
        cost_estimate=pl.CostEstimate(
            flops=products,
            bytes_accessed=12 * POS * WIDTH,
            transcendentals=4 * HEADS * POS * POS,
        ),
        name="attention",
    )(*(array.reshape(POS, WIDTH) for array in arrays))
    grads = pl.pallas_call(
        write_out,
        out_shape=[jax.ShapeDtypeStruct((POS, WIDTH), jnp.bfloat16)] * 5,
        in_specs=[array] * 5,
        out_specs=[array] * 5,
        scratch_shapes=[dma((5,))],
        compiler_params=pltpu.CompilerParams(vmem_limit_bytes=1 << 20),
        cost_estimate=pl.CostEstimate(
            flops=0, bytes_accessed=20 * POS * WIDTH, transcendentals=0
        ),
        name="write_out",
    )(*grads)
    return tuple(entry[None] for entry in grads)


def solution(mesh):
    spec = P(("dp", "seq"), None, None)
    return jax.shard_map(
        shards, mesh=mesh, in_specs=(spec,) * 6, out_specs=(spec,) * 5, check_vma=False
    )
```

```python
import functools
import math

import jax
import jax.numpy as jnp
from jax import lax
from jax.experimental import pallas as pl
from jax.experimental.pallas import tpu as pltpu
from jax.sharding import PartitionSpec as P

HEADS = 16
HEAD_DIM = 128
SCALE = HEAD_DIM**-0.5
SCALE2 = SCALE * math.log2(math.e)
MESH = pl.DeviceIdType.MESH

FRAMES = 32
POS = 512
OWN = POS // FRAMES
WIDTH = HEADS * HEAD_DIM
CHUNKS = 8
COLS = WIDTH // CHUNKS
CHUNK_HEADS = HEADS // CHUNKS


def product(left, right, contract):
    return lax.dot_general(left, right, (contract, ((), ())), preferred_element_type=jnp.float32)


def plain(left, right):
    return product(left, right, ((1,), (0,)))


def against(left, right):
    return product(left, right, ((1,), (1,)))


def probabilities(queries, key_rows, bias=None):
    scores = against(key_rows, queries) * SCALE2
    if bias is not None:
        scores = (scores.reshape(FRAMES, OWN, POS) + bias[None]).reshape(POS, POS)
    scores = jnp.exp2(scores - jnp.max(scores, axis=0, keepdims=True))
    return scores * (1.0 / jnp.sum(scores, axis=0, keepdims=True))


def score_backward(queries, key_rows, values, weights, upstream):
    weight_grads = against(values, upstream)
    weighted = weights * weight_grads
    score_grads = weighted - weights * jnp.sum(weighted, axis=0, keepdims=True)
    score_grads = score_grads.astype(jnp.bfloat16)
    key_grads = plain(score_grads, queries) * SCALE
    query_grads = (plain(key_rows.T, score_grads) * SCALE).T
    return query_grads.astype(jnp.bfloat16), key_grads.astype(jnp.bfloat16)


def value_backward(weights, upstream):
    return plain(weights.astype(jnp.bfloat16), upstream).astype(jnp.bfloat16)


def kernel(
    q_space, k_space, v_space, q_time, k_time, grad_out,
    gq_space, gk_space, gv_space, gq_time, gk_time,
    sq, sk, sv, so, gs, held, made, bias,
    load_sem, send_sem, qkg_sem, so_sem, gs_sem, back_sem,
):
    seq, dp = lax.axis_index("seq"), lax.axis_index("dp")
    my_rows = pl.ds(pl.multiple_of(seq * OWN, OWN), OWN)

    def columns(chunk):
        return pl.ds(pl.multiple_of(chunk * COLS, COLS), COLS)

    def head_columns(head):
        return pl.ds(pl.multiple_of(head * HEAD_DIM, HEAD_DIM), HEAD_DIM)

    def peer_of(step):
        y = lax.rem(seq // 8 + step // 8, 4)
        z = lax.rem(seq // 4 + step // 4, 2)
        x = lax.rem(seq + step, 4)
        return y * 8 + z * 4 + x

    def rows_of(device):
        return pl.ds(pl.multiple_of(device * OWN, OWN), OWN)

    def spread(chunk, source, target, sent, landed):
        cols = columns(chunk)

        def one(step, carry):
            peer = peer_of(step)
            pltpu.make_async_remote_copy(
                src_ref=source.at[rows_of(peer), cols],
                dst_ref=target.at[my_rows, cols],
                send_sem=sent,
                recv_sem=landed,
                device_id=(dp, peer),
                device_id_type=MESH,
            ).start()
            return carry

        lax.fori_loop(1, FRAMES, one, 0)
        pltpu.make_async_copy(source.at[my_rows, cols], target.at[my_rows, cols], landed).start()

    def wait_for(ref, sem):
        pltpu.make_async_copy(ref, ref, sem).wait()

    barrier = pltpu.get_barrier_semaphore()

    for step in range(1, FRAMES):
        pl.semaphore_signal(barrier, inc=1, device_id=(dp, peer_of(step)), device_id_type=MESH)
    spatial = ((q_space, sq), (k_space, sk), (v_space, sv))
    for chunk in range(CHUNKS):
        cols = pl.ds(chunk * COLS, COLS)
        for at, (source, target) in enumerate(spatial):
            pltpu.make_async_copy(
                source.at[:, cols], target.at[:, cols], load_sem.at[at, chunk]
            ).start()

    pl.semaphore_wait(barrier, FRAMES - 1)

    def send_inputs(chunk, carry):
        for at, source in enumerate((q_time, k_time, grad_out)):
            spread(chunk, source, held.at[at], send_sem.at[at], qkg_sem.at[at, chunk])
        return carry

    lax.fori_loop(0, CHUNKS, send_inputs, 0)

    rows = lax.broadcasted_iota(jnp.int32, (OWN, POS), 0)
    lanes = lax.broadcasted_iota(jnp.int32, (OWN, POS), 1)
    bias[...] = jnp.where(rows == lanes % OWN, 0.0, -1e30).astype(jnp.float32)

    def space_forward(chunk, carry):
        cols = columns(chunk)
        for at, (source, target) in enumerate(spatial):
            wait_for(target.at[:, cols], load_sem.at[at, chunk])

        def one(index, carry):
            here = head_columns(chunk * CHUNK_HEADS + index)
            weights = probabilities(sq[:, here], sk[:, here]).astype(jnp.bfloat16)
            so[:, here] = plain(sv[:, here].T, weights).T.astype(jnp.bfloat16)
            return carry

        lax.fori_loop(0, CHUNK_HEADS, one, 0)
        spread(chunk, so, held.at[3], send_sem.at[3], so_sem.at[chunk])
        return carry

    lax.fori_loop(0, CHUNKS, space_forward, 0)

    def each_head(chunk, work):
        def one(index, carry):
            work(head_columns(chunk * CHUNK_HEADS + index))
            return carry

        lax.fori_loop(0, CHUNK_HEADS, one, 0)

    def time_weights(here):
        return probabilities(held[0, :, here], held[1, :, here], bias[...])

    def time_values(chunk, carry):
        cols = columns(chunk)
        for at in range(3):
            wait_for(held.at[at, :, cols], qkg_sem.at[at, chunk])

        def work(here):
            made[0, :, here] = value_backward(time_weights(here), held[2, :, here])

        each_head(chunk, work)
        spread(chunk, made.at[0], gs, send_sem.at[4], gs_sem.at[chunk])
        return carry

    lax.fori_loop(0, CHUNKS, time_values, 0)

    def time_scores(chunk, carry):
        wait_for(held.at[3, :, columns(chunk)], so_sem.at[chunk])

        def work(here):
            made[1, :, here], made[2, :, here] = score_backward(
                held[0, :, here], held[1, :, here], held[3, :, here], time_weights(here), held[2, :, here]
            )

        each_head(chunk, work)
        spread(chunk, made.at[1], gq_time, send_sem.at[5], back_sem.at[0])
        spread(chunk, made.at[2], gk_time, send_sem.at[6], back_sem.at[1])
        return carry

    lax.fori_loop(0, CHUNKS, time_scores, 0)

    def space_back(chunk, carry):
        wait_for(gs.at[:, columns(chunk)], gs_sem.at[chunk])

        def work(here):
            weights = probabilities(sq[:, here], sk[:, here])
            gv_space[:, here] = value_backward(weights, gs[:, here])
            gq_space[:, here], gk_space[:, here] = score_backward(
                sq[:, here], sk[:, here], sv[:, here], weights, gs[:, here]
            )

        each_head(chunk, work)
        return carry

    lax.fori_loop(0, CHUNKS, space_back, 0)

    sent = POS - OWN
    for at in range(7):
        wait_for(held.at[0, pl.ds(0, sent)], send_sem.at[at])
    wait_for(gq_time, back_sem.at[0])
    wait_for(gk_time, back_sem.at[1])


def write_out(*refs):
    sources, targets, sem = refs[:5], refs[5:10], refs[10]
    copies = [
        pltpu.make_async_copy(source, target, sem.at[at])
        for at, (source, target) in enumerate(zip(sources, targets))
    ]
    for copy in copies:
        copy.start()
    for copy in copies:
        copy.wait()


def shards(*arrays):
    array = pl.BlockSpec(memory_space=pl.ANY)
    whole = pltpu.VMEM((POS, WIDTH), jnp.bfloat16)
    dma = pltpu.SemaphoreType.DMA
    products = 12 * 2 * HEADS * POS * POS * HEAD_DIM
    grads = pl.pallas_call(
        kernel,
        out_shape=[pltpu.VMEM((POS, WIDTH), jnp.bfloat16)] * 5,
        in_specs=[array] * 6,
        out_specs=[pl.BlockSpec(memory_space=pltpu.VMEM)] * 5,
        scratch_shapes=[
            whole, whole, whole, whole, whole,
            pltpu.VMEM((4, POS, WIDTH), jnp.bfloat16),
            pltpu.VMEM((3, POS, WIDTH), jnp.bfloat16),
            pltpu.VMEM((OWN, POS), jnp.float32),
            dma((3, CHUNKS)), dma((7,)), dma((3, CHUNKS)), dma((CHUNKS,)), dma((CHUNKS,)), dma((2,)),
        ],
        compiler_params=pltpu.CompilerParams(collective_id=0, has_side_effects=True, vmem_limit_bytes=46 << 20),
        cost_estimate=pl.CostEstimate(
            flops=products,
            bytes_accessed=12 * POS * WIDTH,
            transcendentals=4 * HEADS * POS * POS,
        ),
        name="attention",
    )(*(array.reshape(POS, WIDTH) for array in arrays))
    grads = pl.pallas_call(
        write_out,
        out_shape=[jax.ShapeDtypeStruct((POS, WIDTH), jnp.bfloat16)] * 5,
        in_specs=[array] * 5,
        out_specs=[array] * 5,
        scratch_shapes=[dma((5,))],
        compiler_params=pltpu.CompilerParams(vmem_limit_bytes=1 << 20),
        cost_estimate=pl.CostEstimate(
            flops=0, bytes_accessed=20 * POS * WIDTH, transcendentals=0
        ),
        name="write_out",
    )(*grads)
    return tuple(entry[None] for entry in grads)


def solution(mesh):
    spec = P(("dp", "seq"), None, None)
    return jax.shard_map(
        shards, mesh=mesh, in_specs=(spec,) * 6, out_specs=(spec,) * 5, check_vma=False
    )
```

```python
import functools
import math

import jax
import jax.numpy as jnp
from jax import lax
from jax.experimental import pallas as pl
from jax.experimental.pallas import tpu as pltpu
from jax.sharding import PartitionSpec as P

HEADS = 16
HEAD_DIM = 128
SCALE = HEAD_DIM**-0.5
SCALE2 = SCALE * math.log2(math.e)
MESH = pl.DeviceIdType.MESH

FRAMES = 32
POS = 512
OWN = POS // FRAMES
WIDTH = HEADS * HEAD_DIM
CHUNKS = 4
COLS = WIDTH // CHUNKS
CHUNK_HEADS = HEADS // CHUNKS


def product(left, right, contract):
    return lax.dot_general(left, right, (contract, ((), ())), preferred_element_type=jnp.float32)


def plain(left, right):
    return product(left, right, ((1,), (0,)))


def against(left, right):
    return product(left, right, ((1,), (1,)))


def probabilities(queries, key_rows, bias=None):
    scores = against(key_rows, queries) * SCALE2
    if bias is not None:
        scores = (scores.reshape(FRAMES, OWN, POS) + bias[None]).reshape(POS, POS)
    scores = jnp.exp2(scores - jnp.max(scores, axis=0, keepdims=True))
    return scores * (1.0 / jnp.sum(scores, axis=0, keepdims=True))


def score_backward(queries, key_rows, values, weights, upstream):
    weight_grads = against(values, upstream)
    weighted = weights * weight_grads
    score_grads = weighted - weights * jnp.sum(weighted, axis=0, keepdims=True)
    score_grads = score_grads.astype(jnp.bfloat16)
    key_grads = plain(score_grads, queries) * SCALE
    query_grads = (plain(key_rows.T, score_grads) * SCALE).T
    return query_grads.astype(jnp.bfloat16), key_grads.astype(jnp.bfloat16)


def value_backward(weights, upstream):
    return plain(weights.astype(jnp.bfloat16), upstream).astype(jnp.bfloat16)


def kernel(
    q_space, k_space, v_space, q_time, k_time, grad_out,
    gq_space, gk_space, gv_space, gq_time, gk_time,
    sq, sk, sv, so, gs, held, made, bias,
    load_sem, send_sem, qkg_sem, so_sem, gs_sem, back_sem,
):
    seq, dp = lax.axis_index("seq"), lax.axis_index("dp")
    my_rows = pl.ds(pl.multiple_of(seq * OWN, OWN), OWN)

    def columns(chunk):
        return pl.ds(pl.multiple_of(chunk * COLS, COLS), COLS)

    def head_columns(head):
        return pl.ds(pl.multiple_of(head * HEAD_DIM, HEAD_DIM), HEAD_DIM)

    def peer_of(step):
        y = lax.rem(seq // 8 + step // 8, 4)
        z = lax.rem(seq // 4 + step // 4, 2)
        x = lax.rem(seq + step, 4)
        return y * 8 + z * 4 + x

    def rows_of(device):
        return pl.ds(pl.multiple_of(device * OWN, OWN), OWN)

    def spread(chunk, source, target, sent, landed):
        cols = columns(chunk)

        def one(step, carry):
            peer = peer_of(step)
            pltpu.make_async_remote_copy(
                src_ref=source.at[rows_of(peer), cols],
                dst_ref=target.at[my_rows, cols],
                send_sem=sent,
                recv_sem=landed,
                device_id=(dp, peer),
                device_id_type=MESH,
            ).start()
            return carry

        lax.fori_loop(1, FRAMES, one, 0)
        pltpu.make_async_copy(source.at[my_rows, cols], target.at[my_rows, cols], landed).start()

    def wait_for(ref, sem):
        pltpu.make_async_copy(ref, ref, sem).wait()

    barrier = pltpu.get_barrier_semaphore()

    for step in range(1, FRAMES):
        pl.semaphore_signal(barrier, inc=1, device_id=(dp, peer_of(step)), device_id_type=MESH)
    spatial = ((q_space, sq), (k_space, sk), (v_space, sv))
    for chunk in range(CHUNKS):
        cols = pl.ds(chunk * COLS, COLS)
        for at, (source, target) in enumerate(spatial):
            pltpu.make_async_copy(
                source.at[:, cols], target.at[:, cols], load_sem.at[at, chunk]
            ).start()

    pl.semaphore_wait(barrier, FRAMES - 1)

    def send_inputs(chunk):
        for at, source in enumerate((q_time, k_time, grad_out)):
            spread(chunk, source, held.at[at], send_sem.at[at], qkg_sem.at[at, chunk])

    rows = lax.broadcasted_iota(jnp.int32, (OWN, POS), 0)
    lanes = lax.broadcasted_iota(jnp.int32, (OWN, POS), 1)
    bias[...] = jnp.where(rows == lanes % OWN, 0.0, -1e30).astype(jnp.float32)

    def space_forward(chunk, carry):
        send_inputs(chunk)
        cols = columns(chunk)
        for at, (source, target) in enumerate(spatial):
            wait_for(target.at[:, cols], load_sem.at[at, chunk])

        def one(index, carry):
            here = head_columns(chunk * CHUNK_HEADS + index)
            weights = probabilities(sq[:, here], sk[:, here]).astype(jnp.bfloat16)
            so[:, here] = plain(sv[:, here].T, weights).T.astype(jnp.bfloat16)
            return carry

        lax.fori_loop(0, CHUNK_HEADS, one, 0)
        spread(chunk, so, held.at[3], send_sem.at[3], so_sem.at[chunk])
        return carry

    lax.fori_loop(0, CHUNKS, space_forward, 0)

    def each_head(chunk, work):
        def one(index, carry):
            work(head_columns(chunk * CHUNK_HEADS + index))
            return carry

        lax.fori_loop(0, CHUNK_HEADS, one, 0)

    def time_weights(here):
        return probabilities(held[0, :, here], held[1, :, here], bias[...])

    def time_values(chunk, carry):
        cols = columns(chunk)
        for at in range(3):
            wait_for(held.at[at, :, cols], qkg_sem.at[at, chunk])

        def work(here):
            made[0, :, here] = value_backward(time_weights(here), held[2, :, here])

        each_head(chunk, work)
        spread(chunk, made.at[0], gs, send_sem.at[4], gs_sem.at[chunk])
        return carry

    lax.fori_loop(0, CHUNKS, time_values, 0)

    def time_scores(chunk, carry):
        wait_for(held.at[3, :, columns(chunk)], so_sem.at[chunk])

        def work(here):
            made[1, :, here], made[2, :, here] = score_backward(
                held[0, :, here], held[1, :, here], held[3, :, here], time_weights(here), held[2, :, here]
            )

        each_head(chunk, work)
        spread(chunk, made.at[1], gq_time, send_sem.at[5], back_sem.at[0])
        spread(chunk, made.at[2], gk_time, send_sem.at[6], back_sem.at[1])
        return carry

    lax.fori_loop(0, CHUNKS, time_scores, 0)

    def space_back(chunk, carry):
        wait_for(gs.at[:, columns(chunk)], gs_sem.at[chunk])

        def work(here):
            weights = probabilities(sq[:, here], sk[:, here])
            gv_space[:, here] = value_backward(weights, gs[:, here])
            gq_space[:, here], gk_space[:, here] = score_backward(
                sq[:, here], sk[:, here], sv[:, here], weights, gs[:, here]
            )

        each_head(chunk, work)
        return carry

    lax.fori_loop(0, CHUNKS, space_back, 0)

    sent = POS - OWN
    for at in range(7):
        wait_for(held.at[0, pl.ds(0, sent)], send_sem.at[at])
    wait_for(gq_time, back_sem.at[0])
    wait_for(gk_time, back_sem.at[1])


def write_out(*refs):
    sources, targets, sem = refs[:5], refs[5:10], refs[10]
    copies = [
        pltpu.make_async_copy(source, target, sem.at[at])
        for at, (source, target) in enumerate(zip(sources, targets))
    ]
    for copy in copies:
        copy.start()
    for copy in copies:
        copy.wait()


def shards(*arrays):
    array = pl.BlockSpec(memory_space=pl.ANY)
    whole = pltpu.VMEM((POS, WIDTH), jnp.bfloat16)
    dma = pltpu.SemaphoreType.DMA
    products = 12 * 2 * HEADS * POS * POS * HEAD_DIM
    grads = pl.pallas_call(
        kernel,
        out_shape=[pltpu.VMEM((POS, WIDTH), jnp.bfloat16)] * 5,
        in_specs=[array] * 6,
        out_specs=[pl.BlockSpec(memory_space=pltpu.VMEM)] * 5,
        scratch_shapes=[
            whole, whole, whole, whole, whole,
            pltpu.VMEM((4, POS, WIDTH), jnp.bfloat16),
            pltpu.VMEM((3, POS, WIDTH), jnp.bfloat16),
            pltpu.VMEM((OWN, POS), jnp.float32),
            dma((3, CHUNKS)), dma((7,)), dma((3, CHUNKS)), dma((CHUNKS,)), dma((CHUNKS,)), dma((2,)),
        ],
        compiler_params=pltpu.CompilerParams(collective_id=0, has_side_effects=True, vmem_limit_bytes=46 << 20),
        cost_estimate=pl.CostEstimate(
            flops=products,
            bytes_accessed=12 * POS * WIDTH,
            transcendentals=4 * HEADS * POS * POS,
        ),
        name="attention",
    )(*(array.reshape(POS, WIDTH) for array in arrays))
    grads = pl.pallas_call(
        write_out,
        out_shape=[jax.ShapeDtypeStruct((POS, WIDTH), jnp.bfloat16)] * 5,
        in_specs=[array] * 5,
        out_specs=[array] * 5,
        scratch_shapes=[dma((5,))],
        compiler_params=pltpu.CompilerParams(vmem_limit_bytes=1 << 20),
        cost_estimate=pl.CostEstimate(
            flops=0, bytes_accessed=20 * POS * WIDTH, transcendentals=0
        ),
        name="write_out",
    )(*grads)
    return tuple(entry[None] for entry in grads)


def solution(mesh):
    spec = P(("dp", "seq"), None, None)
    return jax.shard_map(
        shards, mesh=mesh, in_specs=(spec,) * 6, out_specs=(spec,) * 5, check_vma=False
    )
```

```python
import functools
import math

import jax
import jax.numpy as jnp
from jax import lax
from jax.experimental import pallas as pl
from jax.experimental.pallas import tpu as pltpu
from jax.sharding import PartitionSpec as P

HEADS = 16
HEAD_DIM = 128
SCALE = HEAD_DIM**-0.5
SCALE2 = SCALE * math.log2(math.e)
MESH = pl.DeviceIdType.MESH

FRAMES = 32
POS = 512
OWN = POS // FRAMES
WIDTH = HEADS * HEAD_DIM
CHUNKS = 4
COLS = WIDTH // CHUNKS
CHUNK_HEADS = HEADS // CHUNKS


def product(left, right, contract):
    return lax.dot_general(left, right, (contract, ((), ())), preferred_element_type=jnp.float32)


def plain(left, right):
    return product(left, right, ((1,), (0,)))


def against(left, right):
    return product(left, right, ((1,), (1,)))


def probabilities(queries, key_rows, bias=None):
    scores = against(key_rows, queries) * SCALE2
    if bias is not None:
        scores = (scores.reshape(FRAMES, OWN, POS) + bias[None]).reshape(POS, POS)
    scores = jnp.exp2(scores - jnp.max(scores, axis=0, keepdims=True))
    return scores * (1.0 / jnp.sum(scores, axis=0, keepdims=True))


def score_backward(queries, key_rows, values, weights, upstream):
    weight_grads = against(values, upstream)
    weighted = weights * weight_grads
    score_grads = weighted - weights * jnp.sum(weighted, axis=0, keepdims=True)
    score_grads = score_grads.astype(jnp.bfloat16)
    key_grads = plain(score_grads, queries) * SCALE
    query_grads = (plain(key_rows.T, score_grads) * SCALE).T
    return query_grads.astype(jnp.bfloat16), key_grads.astype(jnp.bfloat16)


def value_backward(weights, upstream):
    return plain(weights.astype(jnp.bfloat16), upstream).astype(jnp.bfloat16)


def kernel(
    q_space, k_space, v_space, q_time, k_time, grad_out,
    gq_space, gk_space, gv_space, gq_time, gk_time,
    sq, sk, sv, so, gs, held, made, bias,
    load_sem, send_sem, qkg_sem, so_sem, gs_sem, back_sem,
):
    seq, dp = lax.axis_index("seq"), lax.axis_index("dp")
    my_rows = pl.ds(pl.multiple_of(seq * OWN, OWN), OWN)

    def columns(chunk):
        return pl.ds(pl.multiple_of(chunk * COLS, COLS), COLS)

    def head_columns(head):
        return pl.ds(pl.multiple_of(head * HEAD_DIM, HEAD_DIM), HEAD_DIM)

    def peer_of(step):
        y = lax.rem(seq // 8 + step // 8, 4)
        z = lax.rem(seq // 4 + step // 4, 2)
        x = lax.rem(seq + step, 4)
        return y * 8 + z * 4 + x

    def rows_of(device):
        return pl.ds(pl.multiple_of(device * OWN, OWN), OWN)

    def spread(chunk, source, target, sent, landed):
        cols = columns(chunk)

        def one(step, carry):
            peer = peer_of(lax.rem(step * 11, FRAMES))
            pltpu.make_async_remote_copy(
                src_ref=source.at[rows_of(peer), cols],
                dst_ref=target.at[my_rows, cols],
                send_sem=sent,
                recv_sem=landed,
                device_id=(dp, peer),
                device_id_type=MESH,
            ).start()
            return carry

        lax.fori_loop(1, FRAMES, one, 0)
        pltpu.make_async_copy(source.at[my_rows, cols], target.at[my_rows, cols], landed).start()

    def wait_for(ref, sem):
        pltpu.make_async_copy(ref, ref, sem).wait()

    barrier = pltpu.get_barrier_semaphore()

    for step in range(1, FRAMES):
        pl.semaphore_signal(barrier, inc=1, device_id=(dp, peer_of(step)), device_id_type=MESH)
    spatial = ((q_space, sq), (k_space, sk), (v_space, sv))
    for chunk in range(CHUNKS):
        cols = pl.ds(chunk * COLS, COLS)
        for at, (source, target) in enumerate(spatial):
            pltpu.make_async_copy(
                source.at[:, cols], target.at[:, cols], load_sem.at[at, chunk]
            ).start()

    pl.semaphore_wait(barrier, FRAMES - 1)

    def send_inputs(chunk):
        for at, source in enumerate((q_time, k_time, grad_out)):
            spread(chunk, source, held.at[at], send_sem.at[at], qkg_sem.at[at, chunk])

    rows = lax.broadcasted_iota(jnp.int32, (OWN, POS), 0)
    lanes = lax.broadcasted_iota(jnp.int32, (OWN, POS), 1)
    bias[...] = jnp.where(rows == lanes % OWN, 0.0, -1e30).astype(jnp.float32)

    def space_forward(chunk, carry):
        send_inputs(chunk)
        cols = columns(chunk)
        for at, (source, target) in enumerate(spatial):
            wait_for(target.at[:, cols], load_sem.at[at, chunk])

        def one(index, carry):
            here = head_columns(chunk * CHUNK_HEADS + index)
            weights = probabilities(sq[:, here], sk[:, here]).astype(jnp.bfloat16)
            so[:, here] = plain(sv[:, here].T, weights).T.astype(jnp.bfloat16)
            return carry

        lax.fori_loop(0, CHUNK_HEADS, one, 0)
        spread(chunk, so, held.at[3], send_sem.at[3], so_sem.at[chunk])
        return carry

    lax.fori_loop(0, CHUNKS, space_forward, 0)

    def each_head(chunk, work):
        def one(index, carry):
            work(head_columns(chunk * CHUNK_HEADS + index))
            return carry

        lax.fori_loop(0, CHUNK_HEADS, one, 0)

    def time_weights(here):
        return probabilities(held[0, :, here], held[1, :, here], bias[...])

    def time_values(chunk, carry):
        cols = columns(chunk)
        for at in range(3):
            wait_for(held.at[at, :, cols], qkg_sem.at[at, chunk])

        def work(here):
            made[0, :, here] = value_backward(time_weights(here), held[2, :, here])

        each_head(chunk, work)
        spread(chunk, made.at[0], gs, send_sem.at[4], gs_sem.at[chunk])
        return carry

    lax.fori_loop(0, CHUNKS, time_values, 0)

    def time_scores(chunk, carry):
        wait_for(held.at[3, :, columns(chunk)], so_sem.at[chunk])

        def work(here):
            made[1, :, here], made[2, :, here] = score_backward(
                held[0, :, here], held[1, :, here], held[3, :, here], time_weights(here), held[2, :, here]
            )

        each_head(chunk, work)
        spread(chunk, made.at[1], gq_time, send_sem.at[5], back_sem.at[0])
        spread(chunk, made.at[2], gk_time, send_sem.at[6], back_sem.at[1])
        return carry

    lax.fori_loop(0, CHUNKS, time_scores, 0)

    def space_back(chunk, carry):
        wait_for(gs.at[:, columns(chunk)], gs_sem.at[chunk])

        def work(here):
            weights = probabilities(sq[:, here], sk[:, here])
            gv_space[:, here] = value_backward(weights, gs[:, here])
            gq_space[:, here], gk_space[:, here] = score_backward(
                sq[:, here], sk[:, here], sv[:, here], weights, gs[:, here]
            )

        each_head(chunk, work)
        return carry

    lax.fori_loop(0, CHUNKS, space_back, 0)

    sent = POS - OWN
    for at in range(7):
        wait_for(held.at[0, pl.ds(0, sent)], send_sem.at[at])
    wait_for(gq_time, back_sem.at[0])
    wait_for(gk_time, back_sem.at[1])


def write_out(*refs):
    sources, targets, sem = refs[:5], refs[5:10], refs[10]
    copies = [
        pltpu.make_async_copy(source, target, sem.at[at])
        for at, (source, target) in enumerate(zip(sources, targets))
    ]
    for copy in copies:
        copy.start()
    for copy in copies:
        copy.wait()


def shards(*arrays):
    array = pl.BlockSpec(memory_space=pl.ANY)
    whole = pltpu.VMEM((POS, WIDTH), jnp.bfloat16)
    dma = pltpu.SemaphoreType.DMA
    products = 12 * 2 * HEADS * POS * POS * HEAD_DIM
    grads = pl.pallas_call(
        kernel,
        out_shape=[pltpu.VMEM((POS, WIDTH), jnp.bfloat16)] * 5,
        in_specs=[array] * 6,
        out_specs=[pl.BlockSpec(memory_space=pltpu.VMEM)] * 5,
        scratch_shapes=[
            whole, whole, whole, whole, whole,
            pltpu.VMEM((4, POS, WIDTH), jnp.bfloat16),
            pltpu.VMEM((3, POS, WIDTH), jnp.bfloat16),
            pltpu.VMEM((OWN, POS), jnp.float32),
            dma((3, CHUNKS)), dma((7,)), dma((3, CHUNKS)), dma((CHUNKS,)), dma((CHUNKS,)), dma((2,)),
        ],
        compiler_params=pltpu.CompilerParams(collective_id=0, has_side_effects=True, vmem_limit_bytes=46 << 20),
        cost_estimate=pl.CostEstimate(
            flops=products,
            bytes_accessed=12 * POS * WIDTH,
            transcendentals=4 * HEADS * POS * POS,
        ),
        name="attention",
    )(*(array.reshape(POS, WIDTH) for array in arrays))
    grads = pl.pallas_call(
        write_out,
        out_shape=[jax.ShapeDtypeStruct((POS, WIDTH), jnp.bfloat16)] * 5,
        in_specs=[array] * 5,
        out_specs=[array] * 5,
        scratch_shapes=[dma((5,))],
        compiler_params=pltpu.CompilerParams(vmem_limit_bytes=1 << 20),
        cost_estimate=pl.CostEstimate(
            flops=0, bytes_accessed=20 * POS * WIDTH, transcendentals=0
        ),
        name="write_out",
    )(*grads)
    return tuple(entry[None] for entry in grads)


def solution(mesh):
    spec = P(("dp", "seq"), None, None)
    return jax.shard_map(
        shards, mesh=mesh, in_specs=(spec,) * 6, out_specs=(spec,) * 5, check_vma=False
    )
```
